32 devices in a mesh: grp: 2 (over y), ep: 8 (over z, x), dp: 2 (over core).
Axes of the slice: x: 2, y: 2, z: 4, core: 2. Of those that a mesh axis runs over, the one named last changes fastest.
Arguments:
- tokens: bfloat16 [4096, 2048], P(('grp', 'ep', 'dp')), parts along dimension 0, may hold values from -6 to 6
- expert_ids: int32 [4096, 8], P(('grp', 'ep', 'dp')), parts along dimension 0, may hold values from 0 to 15, all different within a row; in each aligned block of 128 rows (0 to 127, 128 to 255, ...) at most 80 rows name the same one
- route_gates: float32 [4096, 8], P(('grp', 'ep', 'dp')), parts along dimension 0, may hold values from 0.2 to 1
- expert_in: bfloat16 [32, 2048, 1536], P(('grp', 'ep', 'dp')), parts along dimension 0, may hold values from -0.125 to 0.125
- expert_out: bfloat16 [32, 768, 2048], P(('grp', 'ep', 'dp')), parts along dimension 0, may hold values from -0.21875 to 0.21875
- old_place: int32 [16], replicated, may hold values from 0 to 15, as said below
- new_place: int32 [16], replicated, may hold values from 0 to 15, as said below
Outputs:
- moe_out: bfloat16 [4096, 2048], P(('grp', 'ep', 'dp')), parts along dimension 0
The draws below stay inside these ranges and needn't reach their ends.
There are 2 independent parts, one for each index of `grp`. The reference program is written for one: setup_inputs(seed, part) draws one part's arguments, and reference() takes and returns one part's arrays. A program takes and returns all parts, laid end to end along the dimension named above; an argument that names none is the same for every part. Nothing has to cross between parts.
Inputs may be any that keep to these rules, and one draw needn't show every extreme that they name: `expert_ids`: each row names 8 different experts; in the 128 rows of one device no expert is named by more than 80 rows, a bound that some block reaches. `old_place`: A permutation of the 16 devices. `new_place`: a permutation of the 16 devices with new_place[e] != old_place[e] for every expert e.
All inputs are finite; a program needn't handle non-finite values.
Results may differ from the reference program's by a relative error of at most 0.0058.
Values may be sent and summed in bfloat16 or wider, within the bound.
No kernel may reach another device: no remote copies, remote signals or barrier semaphores. Data moves between devices by JAX's collectives and lax.ppermute only.
A program may use at most 128 MiB of HBM per device.

```python
import math
import jax
import jax.numpy as jnp
import numpy as np
from jax import lax

D = 2048
FF = 768
TOP = 8
TOK_DEV = 128
BLOCK = 128
EXPERTS = 16
TOKENS = 2048
CAP = 80
SERVE_BLOCKS = 9
N_EP = 8
N_DP = 2


def placement_tables(key):
    first_key = jax.random.fold_in(key, 11)
    second_key = jax.random.fold_in(key, 23)
    old_order = jax.random.permutation(first_key, EXPERTS).astype(jnp.int32)
    shuffle = jax.random.permutation(second_key, EXPERTS).astype(jnp.int32)
    inverse = jnp.argsort(shuffle, stable=True).astype(jnp.int32)
    cycled = shuffle[(inverse + 1) % EXPERTS]
    return (old_order, old_order[cycled])


def draw_old_place(key, part):
    return placement_tables(key)[0]


def draw_new_place(key, part):
    return placement_tables(key)[1]


def block_scale(key, extent, shards, low, top_value):
    loudness = 1.0
    for dim, parts in shards:
        steps = jax.random.uniform(jax.random.fold_in(jax.random.fold_in(key, 6), dim), (parts,), jnp.float32, low / len(shards), top_value / len(shards))
        loudness = loudness * jnp.repeat(jnp.exp(steps), extent[dim] // parts).reshape((-1,) + (1,) * (len(extent) - 1 - dim))
    return loudness


def shared_out(own_key, own, number, rows, amount, top, most, skew):
    order = jax.random.permutation(own_key, amount)
    crowded, ordinary = shares(amount, rows * top, most, skew, True), shares(amount, rows * top, most, skew, False)
    places = jnp.arange(amount)

    def named(tallies, turn):
        used = int((tallies > 0).sum())
        fixed = max(1, used // 4)
        moved = fixed + (places - fixed + turn * (used - fixed)) % max(1, amount - fixed)
        return jnp.zeros((amount,), jnp.int32).at[order[jnp.where(places < fixed, places, moved)]].set(jnp.asarray(tallies, jnp.int32))

    tallies = jnp.where(number % 4 == 0, named(crowded, number // 4), named(ordinary, number - number // 4 - 1))
    mixed = jax.random.permutation(jax.random.fold_in(own, 3), amount)
    source_of, sink = mixed[0:amount // 2 * 2:2], mixed[1:amount // 2 * 2:2]
    room = jnp.minimum(tallies[source_of] - 1, most - tallies[sink]) // 2
    room = jnp.where((source_of == order[0]) | (sink == order[0]) | (tallies[sink] == 0), 0, jnp.maximum(room, 0))
    moved = jax.random.randint(jax.random.fold_in(own, 4), (amount // 2,), 0, 1 << 20) % (room + 1)
    tallies = tallies.at[source_of].add(-moved).at[sink].add(moved)
    members = jnp.searchsorted(jnp.cumsum(tallies), jnp.arange(rows * top), side="right").astype(jnp.int32)
    grid = members.reshape(top, rows).T
    grid = grid[jax.random.permutation(jax.random.fold_in(own, 1), rows)]
    turn = jax.random.randint(jax.random.fold_in(own, 2), (rows, 1), 0, top)
    return jnp.take_along_axis(grid, (jnp.arange(top)[None, :] + turn) % top, axis=1)


def shares(number_of, total, reach, lean, full):
    loads = [(1 << 20) // math.isqrt(standing ** lean) + 1 for standing in range(1, number_of + 1)]
    largest = reach if full else min(reach, max(-(-total // number_of), total * loads[0] // sum(loads)))
    least = 1 if total - largest >= number_of - 1 else 0
    holding, spare = [largest] + [least] * (number_of - 1), total - largest - least * (number_of - 1)
    while spare > 0:
        movable = [i for i in range(1, number_of) if holding[i] < largest] or [i for i in range(1, number_of) if holding[i] < reach]
        mass, remaining = sum([loads[i] for i in movable]), spare
        for i in movable:
            addition = min(reach - holding[i], max(1, remaining * loads[i] // mass), spare)
            holding[i] = holding[i] + addition
            spare = spare - addition
    return np.array(holding)


def noise(stream_key, dims, width, limit, split=(), kind=jnp.bfloat16):
    drawn = jax.random.normal(stream_key, dims, jnp.float32) * width
    if len(split) > 0:
        drawn = block_scale(stream_key, dims, split, -0.22, 0.18) * drawn
    return jnp.clip(drawn, min=-limit, max=limit).astype(kind)


def setup_inputs(seed: int = 0, part: int = 0) -> dict:
    arg_keys = jax.random.split(jax.random.key(seed), 8)
    part_keys = jax.random.split(jax.random.fold_in(arg_keys[7], part), 8)
    tokens = noise(part_keys[0], (TOKENS, D), 1.0, 6.0, ((0, 16),))
    expert_ids_keys = jax.random.split(jax.random.fold_in(part_keys[1], 1), TOKENS // TOK_DEV)
    expert_ids_turns = jax.random.permutation(jax.random.fold_in(part_keys[1], 3), TOKENS // TOK_DEV)
    expert_ids = jax.vmap(lambda own, number: shared_out(jax.random.fold_in(part_keys[1], 2), own, number, TOK_DEV, EXPERTS, TOP, CAP, 2))(expert_ids_keys, expert_ids_turns).reshape((TOKENS, TOP))
    route_gates = jnp.clip(0.2 + 0.8 * jax.random.uniform(part_keys[2], (TOKENS, TOP), jnp.float32) ** block_scale(part_keys[2], (TOKENS, TOP), ((0, 16),), -0.2, 0.2), 0.2, 1.0)
    expert_in = noise(part_keys[3], (EXPERTS, D, 2 * FF), D ** -0.5, 0.125, ((0, 16),))
    expert_out = noise(part_keys[4], (EXPERTS, FF, D), FF ** -0.5, 0.21875, ((0, 16),))
    old_place = draw_old_place(jax.random.fold_in(arg_keys[7], 71), part)
    new_place = draw_new_place(jax.random.fold_in(arg_keys[7], 71), part)
    return {"tokens": tokens, "expert_ids": expert_ids, "route_gates": route_gates, "expert_in": expert_in, "expert_out": expert_out, "old_place": old_place, "new_place": new_place}


def expert_rows(token_rows, in_weights, out_weights):
    projected = jnp.dot(token_rows, in_weights, preferred_element_type=jnp.float32)
    gate_part = projected[:, :FF]
    up_part = projected[:, FF:]
    hidden = (jax.nn.silu(gate_part) * up_part).astype(jnp.bfloat16)
    return jnp.dot(hidden, out_weights, preferred_element_type=jnp.float32).astype(jnp.bfloat16)


def reference(tokens, expert_ids, route_gates, expert_in, expert_out, old_place, new_place):
    devices = N_EP * N_DP
    assigns = TOK_DEV * TOP
    role_rows = N_EP * CAP
    experts = jnp.arange(devices, dtype=jnp.int32)
    flat_ids = expert_ids.reshape(devices, assigns)
    home_src = (experts % N_DP) == 0
    server = jnp.where(home_src[:, None], old_place[flat_ids], new_place[flat_ids]).astype(jnp.int32)
    onehot = (server[:, :, None] == experts[None, None, :]).astype(jnp.int32)
    local_rank = jnp.sum((jnp.cumsum(onehot, axis=1) - onehot) * onehot, axis=2)
    counts = jnp.sum(onehot, axis=1)
    home_counts = jnp.where(home_src[:, None], counts, 0)
    rep_counts = counts - home_counts
    earlier = jnp.where(home_src[:, None], jnp.cumsum(home_counts, axis=0) - home_counts,
                        jnp.cumsum(rep_counts, axis=0) - rep_counts)
    slot_rank = (jnp.take_along_axis(earlier, server, axis=1) + local_rank).astype(jnp.int32)
    home_blocks = ((jnp.sum(home_counts, axis=0) + BLOCK - 1) // BLOCK).astype(jnp.int32)
    position = jnp.where(home_src[:, None], slot_rank, home_blocks[server] * BLOCK + slot_rank)
    served = position < SERVE_BLOCKS * BLOCK
    role_index = jnp.where(home_src[:, None], 0, 1) * jnp.ones((devices, assigns), jnp.int32)
    entry_ids = jnp.arange(devices * assigns, dtype=jnp.int32).reshape(devices, assigns)
    entries = jnp.full((devices, 2, role_rows), -1, jnp.int32).at[server, role_index, slot_rank].set(entry_ids)
    inverse_new = jnp.zeros((devices,), jnp.int32).at[new_place].set(experts)
    replica_slot = old_place[inverse_new].astype(jnp.int32)

    def per_device(device_index):
        chosen = entries[device_index]
        token_rows = jnp.take(tokens, jnp.maximum(chosen, 0) // TOP, axis=0)
        home_out = expert_rows(token_rows[0], expert_in[device_index], expert_out[device_index])
        other = replica_slot[device_index]
        rep_out = expert_rows(token_rows[1], expert_in[other], expert_out[other])
        return jnp.stack([home_out, rep_out])

    outputs = lax.map(per_device, experts)
    flat_out = outputs.reshape(devices * 2 * role_rows, D)
    lookup = ((server * 2 + role_index) * role_rows + slot_rank).reshape(TOKENS, TOP)
    scaled = jnp.where(served.reshape(TOKENS, TOP), route_gates, jnp.float32(0.0))
    summed = jnp.zeros((TOKENS, D), jnp.float32)
    for slot_k in range(TOP):
        picked = jnp.take(flat_out, lookup[:, slot_k], axis=0).astype(jnp.float32)
        summed = summed + picked * scaled[:, slot_k][:, None]
    return summed.astype(jnp.bfloat16)
```

```python
import functools

import jax
import jax.numpy as jnp
from jax import lax
from jax.experimental import pallas as pl
from jax.experimental.pallas import tpu as pltpu
from jax.sharding import PartitionSpec as P

BLOCK = 128
SERVE_BLOCKS = 9


def expert_block(inputs, in_weights, out_weights, hidden_units):
    projected = jnp.dot(inputs, in_weights, preferred_element_type=jnp.float32)
    gate_part = projected[:, :hidden_units]
    up_part = projected[:, hidden_units:]
    hidden = (jax.nn.silu(gate_part) * up_part).astype(jnp.bfloat16)
    return jnp.dot(hidden, out_weights, preferred_element_type=jnp.float32).astype(jnp.bfloat16)


def routed_body(tokens, expert_ids, route_gates, expert_in, expert_out, old_place, new_place):
    ep_size = lax.axis_size("ep")
    dp_size = lax.axis_size("dp")
    devices = ep_size * dp_size
    tok_rows, top_count = expert_ids.shape
    model_width = tokens.shape[1]
    hidden_units = expert_out.shape[1]
    assigns = tok_rows * top_count
    capacity = (5 * assigns + 4 * devices - 1) // (4 * devices)
    serve_rows = SERVE_BLOCKS * BLOCK
    experts = jnp.arange(devices, dtype=jnp.int32)
    flat_ids = expert_ids.reshape(assigns)
    server = jnp.sum(
        jnp.where(flat_ids[:, None] == experts[None, :], old_place[None, :], 0), axis=1
    )
    onehot = (server[:, None] == experts[None, :]).astype(jnp.int32)
    local_rank = jnp.sum((jnp.cumsum(onehot, axis=0) - onehot) * onehot, axis=1)
    counts = jnp.sum(onehot, axis=0)
    slot_index = server * capacity + local_rank
    holder = (
        jnp.full((devices * capacity,), assigns, jnp.int32)
        .at[slot_index]
        .set(jnp.arange(assigns, dtype=jnp.int32))
    )
    token_index = jnp.where(holder < assigns, holder // top_count, tok_rows)
    send_rows = jnp.take(tokens, token_index, axis=0, mode="fill", fill_value=0).reshape(
        devices, capacity, model_width
    )
    recv_rows, recv_counts = (
        lax.all_to_all(send_rows, ("ep", "dp"), split_axis=0, concat_axis=0, tiled=True),
        lax.all_to_all(counts, ("ep", "dp"), split_axis=0, concat_axis=0, tiled=True),
    )
    source_home = experts % dp_size == 0
    home_counts = jnp.where(source_home, recv_counts, 0)
    rep_counts = recv_counts - home_counts
    earlier = jnp.where(
        source_home, jnp.cumsum(home_counts) - home_counts, jnp.cumsum(rep_counts) - rep_counts
    )
    home_blocks = (jnp.sum(home_counts) + BLOCK - 1) // BLOCK
    column = jnp.arange(capacity, dtype=jnp.int32)
    slot_rank = earlier[:, None] + column[None, :]
    present = column[None, :] < recv_counts[:, None]
    own_in = expert_in[0]
    own_out = expert_out[0]
    own_index = lax.axis_index("ep") * dp_size + lax.axis_index("dp")
    held_expert = jnp.sum(jnp.where(old_place == own_index, experts, 0))
    replica_server = jnp.sum(jnp.where(experts == held_expert, new_place, 0))
    all_blocks = lax.all_gather(
        home_blocks.astype(jnp.int32).reshape(1), ("ep", "dp"), axis=0, tiled=True
    )
    replica_blocks = jnp.sum(jnp.where(experts == replica_server, all_blocks, 0))
    base_rows = jnp.minimum(home_blocks, SERVE_BLOCKS) * BLOCK
    served_here = jnp.where(
        source_home[:, None],
        slot_rank < serve_rows,
        replica_blocks * BLOCK + slot_rank < serve_rows,
    )
    live_rows = present & served_here
    pack_rows = 2 * serve_rows
    position = jnp.where(source_home[:, None], slot_rank, base_rows + slot_rank)
    position = jnp.where(live_rows, position, pack_rows).reshape(devices * capacity)
    used_blocks = (jnp.max(jnp.where(position < pack_rows, position + 1, 0)) + BLOCK - 1) // BLOCK
    source_of = (
        jnp.full((pack_rows,), devices * capacity, jnp.int32)
        .at[position]
        .set(jnp.arange(devices * capacity, dtype=jnp.int32), mode="drop")
    )
    packed = jnp.take(
        recv_rows.reshape(devices * capacity, model_width),
        source_of,
        axis=0,
        mode="fill",
        fill_value=0,
    )

    def owner_block(state, block_id):
        inputs = lax.dynamic_slice_in_dim(packed, block_id * BLOCK, BLOCK, 0)
        result = lax.cond(
            block_id < used_blocks,
            lambda rows: expert_block(rows, own_in, own_out, hidden_units),
            lambda rows: jnp.zeros((BLOCK, model_width), jnp.bfloat16),
            inputs,
        )
        return (state, result)

    unused_state, outputs = lax.scan(
        owner_block, jnp.int32(0), jnp.arange(2 * SERVE_BLOCKS, dtype=jnp.int32)
    )
    results = jnp.take(
        outputs.reshape(pack_rows, model_width), position, axis=0, mode="fill", fill_value=0
    ).reshape(devices, capacity, model_width)
    returned = lax.all_to_all(results, ("ep", "dp"), split_axis=0, concat_axis=0, tiled=True)
    picked_rows = jnp.take(returned.reshape(devices * capacity, model_width), slot_index, axis=0)
    weighted = picked_rows.astype(jnp.float32) * route_gates.reshape(assigns)[:, None]
    return jnp.sum(weighted.reshape(tok_rows, top_count, model_width), axis=1).astype(jnp.bfloat16)


def gate_kernel(info_ref, old_ref, new_ref, dense_ref, out_ref):
    devices, _, tok_rows = dense_ref.shape
    own = info_ref[0]
    kind = own % 2
    dense = dense_ref[...]
    which = lax.broadcasted_iota(jnp.int32, dense.shape, 1)
    source_col = lax.broadcasted_iota(jnp.int32, (devices, devices), 0) ^ own
    source_row = lax.broadcasted_iota(jnp.int32, (devices, devices), 1) ^ own
    before = ((source_row < source_col) & (source_row % 2 == kind)).astype(jnp.float32)
    earlier = (
        lax.broadcasted_iota(jnp.int32, (tok_rows, tok_rows), 0)
        < lax.broadcasted_iota(jnp.int32, (tok_rows, tok_rows), 1)
    ).astype(jnp.float32)
    home = (lax.broadcasted_iota(jnp.int32, (devices, tok_rows), 0) ^ own) % 2 == 0

    def holds(server):
        return lax.fori_loop(
            0, devices, lambda e, found: jnp.where(old_ref[e] == server, e, found), 0
        )

    def gates_of(expert):
        return jnp.sum(jnp.where(which == expert, dense, 0.0), axis=1)

    for q in range(2):
        expert = holds(own ^ q)
        gates = gates_of(expert)
        chosen = (gates > 0.0).astype(jnp.float32)
        exact = functools.partial(
            jnp.dot, preferred_element_type=jnp.float32, precision=lax.Precision.HIGHEST
        )
        totals = jnp.sum(chosen, axis=1, keepdims=True)
        ahead = exact(before, jnp.broadcast_to(totals, (devices, tok_rows)))
        rank = exact(chosen, earlier) + ahead
        other = gates_of(holds(new_ref[expert]))
        home_total = jnp.sum(jnp.where(home & (other > 0.0), 1.0, 0.0))
        home_rows = ((home_total.astype(jnp.int32) + (BLOCK - 1)) // BLOCK) * BLOCK
        base = jnp.where(kind == 0, 0, home_rows)
        position = rank.astype(jnp.int32) + base
        served = jnp.where(position < SERVE_BLOCKS * BLOCK, gates, 0.0)
        out_ref[q] = served.T


def expert_kernel(blocks, info_ref, gates_ref, *refs):
    halves = 2 * blocks
    x_refs = refs[:halves]
    weights = refs[halves : halves + 6]
    out_refs = refs[halves + 6 : 2 * halves + 6]
    x_all, total, partial = refs[2 * halves + 6 :]
    q, f = pl.program_id(0), pl.program_id(1)
    last = pl.num_programs(1) - 1
    half = x_refs[0].shape[0]

    @pl.when((q == 0) & (f == 0))
    def _():
        for i in range(halves):
            x_all[i * half : (i + 1) * half, :] = x_refs[i][...]

    def step(gate_ref, up_ref, down_ref):
        x = x_all[...]
        gate = jnp.dot(x, gate_ref[0], preferred_element_type=jnp.float32)
        up = jnp.dot(x, up_ref[0], preferred_element_type=jnp.float32)
        hidden = (gate / (1.0 + jnp.exp(-gate)) * up).astype(jnp.bfloat16)
        part = jnp.dot(hidden, down_ref[0], preferred_element_type=jnp.float32)

        @pl.when(f == 0)
        def _():
            partial[...] = part

        @pl.when(f != 0)
        def _():
            partial[...] += part

    @pl.when(q == 0)
    def _():
        step(*weights[:3])

    @pl.when(q == 1)
    def _():
        step(*weights[3:])

    def column(block):
        table = gates_ref[q]
        lane = lax.broadcasted_iota(jnp.int32, table.shape, 1)
        return jnp.sum(jnp.where(lane == info_ref[block], table, 0.0), axis=1, keepdims=True)

    @pl.when(f == last)
    def _():
        for block in range(blocks):
            rows = slice(block * 2 * half, (block + 1) * 2 * half)
            made = partial[rows, :].astype(jnp.bfloat16).astype(jnp.float32) * column(block)

            @pl.when(q == 0)
            def _():
                total[rows, :] = made

            @pl.when(q == 1)
            def _():
                whole = (total[rows, :] + made).astype(jnp.bfloat16)
                out_refs[2 * block][...] = whole[:half]
                out_refs[2 * block + 1][...] = whole[half:]


def expert_call(halves, columns, gates, weights):
    blocks = len(halves) // 2
    half, width = halves[0].shape
    own_in, own_out, other_in, other_out = weights
    hidden_units = own_out.shape[1]
    tile = 256
    steps = hidden_units // tile
    whole = pl.BlockSpec((half, width), lambda q, f, info: (0, 0))

    def own(shift):
        return lambda q, f, info: (0, 0, jnp.where(q == 0, f, steps - 1) + shift)

    def other(shift):
        return lambda q, f, info: (0, 0, jnp.where(q == 0, 0, f) + shift)

    return pl.pallas_call(
        functools.partial(expert_kernel, blocks),
        out_shape=[jax.ShapeDtypeStruct((half, width), jnp.bfloat16)] * len(halves),
        grid_spec=pltpu.PrefetchScalarGridSpec(
            num_scalar_prefetch=1,
            grid=(2, steps),
            in_specs=[pl.BlockSpec(gates.shape, lambda q, f, info: (0, 0, 0))]
            + [whole] * len(halves)
            + [
                pl.BlockSpec((1, width, tile), own(0)),
                pl.BlockSpec((1, width, tile), own(steps)),
                pl.BlockSpec((1, tile, width), lambda q, f, info: (0, jnp.where(q == 0, f, steps - 1), 0)),
                pl.BlockSpec((1, width, tile), other(0)),
                pl.BlockSpec((1, width, tile), other(steps)),
                pl.BlockSpec((1, tile, width), lambda q, f, info: (0, jnp.where(q == 0, 0, f), 0)),
            ],
            out_specs=[whole] * len(halves),
            scratch_shapes=[
                pltpu.VMEM((half * len(halves), width), jnp.bfloat16),
                pltpu.VMEM((half * len(halves), width), jnp.float32),
                pltpu.VMEM((half * len(halves), width), jnp.float32),
            ],
        ),
        compiler_params=pltpu.CompilerParams(vmem_limit_bytes=40 * 2**20),
        cost_estimate=pl.CostEstimate(
            flops=2 * 2 * half * len(halves) * width * 3 * hidden_units,
            bytes_accessed=2 * 3 * 2 * width * hidden_units,
            transcendentals=0,
        ),
    )(columns, gates, *halves, own_in, own_in, own_out, other_in, other_in, other_out)


def gathered_body(tokens, expert_ids, route_gates, expert_in, expert_out, old_place, new_place):
    ep_size = lax.axis_size("ep")
    devices = ep_size * 2
    tok_rows, top_count = expert_ids.shape
    half = tok_rows // 2
    reach = ep_size // 2
    ring = [*range(0, ep_size, 2), *range(ep_size - 1, 0, -2)]
    ahead = [(ring[i], ring[(i + 1) % ep_size]) for i in range(ep_size)]
    back = [(b, a) for a, b in ahead]
    ep = lax.axis_index("ep")
    own = ep * 2 + lax.axis_index("dp")

    def swap_cores(x):
        return lax.ppermute(x, "dp", [(0, 1), (1, 0)])

    def go(x, way):
        return lax.ppermute(x, "ep", ahead if way > 0 else back)

    ids_t, gates_t = expert_ids.T, route_gates.T
    experts = jnp.arange(devices, dtype=jnp.int32)
    dense = jnp.sum(
        jnp.where(ids_t[None] == experts[:, None, None], gates_t[None], 0.0), axis=1
    )[None]
    dense = jnp.concatenate([dense, swap_cores(dense)])
    bit = 1
    while bit < ep_size:
        pairs = [(i, i ^ bit) for i in range(ep_size)]
        dense = jnp.concatenate([dense, lax.ppermute(dense, "ep", pairs)])
        bit *= 2

    weights = (expert_in, expert_out, swap_cores(expert_in), swap_cores(expert_out))

    held = {0: [tokens[:half], tokens[half:]]}
    for d in range(1, reach):
        held[-d] = [go(x, 1) for x in held[1 - d]]
        held[d] = [go(x, -1) for x in held[d - 1]]
    held[reach] = [go(held[1 - reach][0], 1), go(held[reach - 1][1], -1)]

    gates = pl.pallas_call(
        gate_kernel,
        out_shape=jax.ShapeDtypeStruct((2, tok_rows, devices), jnp.float32),
        in_specs=[pl.BlockSpec(memory_space=pltpu.SMEM)] * 3
        + [pl.BlockSpec(memory_space=pltpu.VMEM)],
    )(own.reshape(1), old_place, new_place, dense)

    ring_at = jnp.array(ring, jnp.int32)
    place = jnp.sum(jnp.where(ring_at == ep, jnp.arange(ep_size, dtype=jnp.int32), 0))

    def columns(distances):
        at = (place + jnp.array(distances, jnp.int32)) % ep_size
        there = jnp.sum(
            jnp.where(at[:, None] == jnp.arange(ep_size)[None], ring_at[None], 0), axis=1
        )
        return ((there ^ ep) * 2).astype(jnp.int32)

    groups = [[0, -1, 1], [-2, 2], [-3, 3, 4]]
    part = {}
    for group in groups:
        outs = expert_call([x for d in group for x in held[d]], columns(group), gates, weights)
        for i, d in enumerate(group):
            part[d] = outs[2 * i : 2 * i + 2]

    def add(*xs):
        return sum(x.astype(jnp.float32) for x in xs).astype(jnp.bfloat16)

    sums = {(1, 0): part[reach][0], (-1, 1): part[reach][1]}
    sums = {k: go(x, k[0]) for k, x in sums.items()}
    for d in range(reach - 1, 0, -1):
        for way in (1, -1):
            for h in (0, 1):
                mine = part[way * d][h]
                so_far = sums.get((way, h))
                sums[way, h] = go(mine if so_far is None else add(so_far, mine), way)
    return jnp.concatenate(
        [add(part[0][h], sums[1, h], sums[-1, h]) for h in (0, 1)]
    )


def solution(mesh):
    placed = (
        P(("grp", "ep", "dp"), None),
        P(("grp", "ep", "dp"), None),
        P(("grp", "ep", "dp"), None),
        P(("grp", "ep", "dp"), None, None),
        P(("grp", "ep", "dp"), None, None),
        P(),
        P(),
    )

    def body(tokens, expert_ids, *rest):
        devices = lax.axis_size("ep") * lax.axis_size("dp")
        gathered = devices <= 2 * expert_ids.shape[1]
        return (gathered_body if gathered else routed_body)(tokens, expert_ids, *rest)

    return jax.shard_map(
        body, mesh=mesh, in_specs=placed, out_specs=P(("grp", "ep", "dp"), None), check_vma=False
    )
```

```python
import functools

import jax
import jax.numpy as jnp
from jax import lax
from jax.experimental import pallas as pl
from jax.experimental.pallas import tpu as pltpu
from jax.sharding import PartitionSpec as P

BLOCK = 128
SERVE_BLOCKS = 9


def expert_block(inputs, in_weights, out_weights, hidden_units):
    projected = jnp.dot(inputs, in_weights, preferred_element_type=jnp.float32)
    gate_part = projected[:, :hidden_units]
    up_part = projected[:, hidden_units:]
    hidden = (jax.nn.silu(gate_part) * up_part).astype(jnp.bfloat16)
    return jnp.dot(hidden, out_weights, preferred_element_type=jnp.float32).astype(jnp.bfloat16)


def routed_body(tokens, expert_ids, route_gates, expert_in, expert_out, old_place, new_place):
    ep_size = lax.axis_size("ep")
    dp_size = lax.axis_size("dp")
    devices = ep_size * dp_size
    tok_rows, top_count = expert_ids.shape
    model_width = tokens.shape[1]
    hidden_units = expert_out.shape[1]
    assigns = tok_rows * top_count
    capacity = (5 * assigns + 4 * devices - 1) // (4 * devices)
    serve_rows = SERVE_BLOCKS * BLOCK
    experts = jnp.arange(devices, dtype=jnp.int32)
    flat_ids = expert_ids.reshape(assigns)
    server = jnp.sum(
        jnp.where(flat_ids[:, None] == experts[None, :], old_place[None, :], 0), axis=1
    )
    onehot = (server[:, None] == experts[None, :]).astype(jnp.int32)
    local_rank = jnp.sum((jnp.cumsum(onehot, axis=0) - onehot) * onehot, axis=1)
    counts = jnp.sum(onehot, axis=0)
    slot_index = server * capacity + local_rank
    holder = (
        jnp.full((devices * capacity,), assigns, jnp.int32)
        .at[slot_index]
        .set(jnp.arange(assigns, dtype=jnp.int32))
    )
    token_index = jnp.where(holder < assigns, holder // top_count, tok_rows)
    send_rows = jnp.take(tokens, token_index, axis=0, mode="fill", fill_value=0).reshape(
        devices, capacity, model_width
    )
    recv_rows, recv_counts = (
        lax.all_to_all(send_rows, ("ep", "dp"), split_axis=0, concat_axis=0, tiled=True),
        lax.all_to_all(counts, ("ep", "dp"), split_axis=0, concat_axis=0, tiled=True),
    )
    source_home = experts % dp_size == 0
    home_counts = jnp.where(source_home, recv_counts, 0)
    rep_counts = recv_counts - home_counts
    earlier = jnp.where(
        source_home, jnp.cumsum(home_counts) - home_counts, jnp.cumsum(rep_counts) - rep_counts
    )
    home_blocks = (jnp.sum(home_counts) + BLOCK - 1) // BLOCK
    column = jnp.arange(capacity, dtype=jnp.int32)
    slot_rank = earlier[:, None] + column[None, :]
    present = column[None, :] < recv_counts[:, None]
    own_in = expert_in[0]
    own_out = expert_out[0]
    own_index = lax.axis_index("ep") * dp_size + lax.axis_index("dp")
    held_expert = jnp.sum(jnp.where(old_place == own_index, experts, 0))
    replica_server = jnp.sum(jnp.where(experts == held_expert, new_place, 0))
    all_blocks = lax.all_gather(
        home_blocks.astype(jnp.int32).reshape(1), ("ep", "dp"), axis=0, tiled=True
    )
    replica_blocks = jnp.sum(jnp.where(experts == replica_server, all_blocks, 0))
    base_rows = jnp.minimum(home_blocks, SERVE_BLOCKS) * BLOCK
    served_here = jnp.where(
        source_home[:, None],
        slot_rank < serve_rows,
        replica_blocks * BLOCK + slot_rank < serve_rows,
    )
    live_rows = present & served_here
    pack_rows = 2 * serve_rows
    position = jnp.where(source_home[:, None], slot_rank, base_rows + slot_rank)
    position = jnp.where(live_rows, position, pack_rows).reshape(devices * capacity)
    used_blocks = (jnp.max(jnp.where(position < pack_rows, position + 1, 0)) + BLOCK - 1) // BLOCK
    source_of = (
        jnp.full((pack_rows,), devices * capacity, jnp.int32)
        .at[position]
        .set(jnp.arange(devices * capacity, dtype=jnp.int32), mode="drop")
    )
    packed = jnp.take(
        recv_rows.reshape(devices * capacity, model_width),
        source_of,
        axis=0,
        mode="fill",
        fill_value=0,
    )

    def owner_block(state, block_id):
        inputs = lax.dynamic_slice_in_dim(packed, block_id * BLOCK, BLOCK, 0)
        result = lax.cond(
            block_id < used_blocks,
            lambda rows: expert_block(rows, own_in, own_out, hidden_units),
            lambda rows: jnp.zeros((BLOCK, model_width), jnp.bfloat16),
            inputs,
        )
        return (state, result)

    unused_state, outputs = lax.scan(
        owner_block, jnp.int32(0), jnp.arange(2 * SERVE_BLOCKS, dtype=jnp.int32)
    )
    results = jnp.take(
        outputs.reshape(pack_rows, model_width), position, axis=0, mode="fill", fill_value=0
    ).reshape(devices, capacity, model_width)
    returned = lax.all_to_all(results, ("ep", "dp"), split_axis=0, concat_axis=0, tiled=True)
    picked_rows = jnp.take(returned.reshape(devices * capacity, model_width), slot_index, axis=0)
    weighted = picked_rows.astype(jnp.float32) * route_gates.reshape(assigns)[:, None]
    return jnp.sum(weighted.reshape(tok_rows, top_count, model_width), axis=1).astype(jnp.bfloat16)


def dense_kernel(ids_ref, gates_ref, out_ref):
    _, experts, tok_rows = out_ref.shape
    expert = lax.broadcasted_iota(jnp.int32, (experts, tok_rows), 0)
    dense = jnp.zeros((experts, tok_rows), jnp.float32)
    for k in range(ids_ref.shape[0]):
        dense += jnp.where(ids_ref[k : k + 1, :] == expert, gates_ref[k : k + 1, :], 0.0)
    out_ref[0] = dense


def join_kernel(mine_ref, theirs_ref, out_ref):
    count = mine_ref.shape[0]
    out_ref[:count] = mine_ref[...]
    out_ref[count:] = theirs_ref[...]


def gate_kernel(info_ref, old_ref, new_ref, mine_ref, theirs_ref, out_ref):
    sources, experts, tok_rows = mine_ref.shape
    own = info_ref[0]
    kind = own % 2
    ep = own // 2
    mine, theirs = mine_ref[...], theirs_ref[...]
    which = lax.broadcasted_iota(jnp.int32, mine.shape, 1)
    source_col = lax.broadcasted_iota(jnp.int32, (sources, sources), 0) ^ ep
    source_row = lax.broadcasted_iota(jnp.int32, (sources, sources), 1) ^ ep
    before = (source_row < source_col).astype(jnp.float32)
    earlier = (
        lax.broadcasted_iota(jnp.int32, (tok_rows, tok_rows), 0)
        < lax.broadcasted_iota(jnp.int32, (tok_rows, tok_rows), 1)
    ).astype(jnp.float32)
    exact = functools.partial(
        jnp.dot, preferred_element_type=jnp.float32, precision=lax.Precision.HIGHEST
    )

    place = jnp.where(ep % 2 == 0, ep // 2, sources - (ep + 1) // 2)
    turn = (place + lax.broadcasted_iota(jnp.int32, (sources, sources), 0)) % sources
    there = jnp.where(2 * turn < sources, 2 * turn, 2 * (sources - turn) - 1)
    in_ring = (
        lax.broadcasted_iota(jnp.int32, (sources, sources), 1) == (there ^ ep)
    ).astype(jnp.float32)

    def holds(server):
        return lax.fori_loop(
            0, experts, lambda e, found: jnp.where(old_ref[e] == server, e, found), 0
        )

    def gates_of(expert, table):
        return jnp.sum(jnp.where(which == expert, table, 0.0), axis=1)

    for q in range(2):
        expert = holds(own ^ q)
        gates = gates_of(expert, mine)
        chosen = (gates > 0.0).astype(jnp.float32)
        totals = jnp.sum(chosen, axis=1, keepdims=True)
        rank = exact(chosen, earlier) + exact(before, jnp.broadcast_to(totals, gates.shape))
        booked = gates_of(holds(new_ref[expert]), theirs)
        home_total = jnp.sum(jnp.where(booked > 0.0, 1.0, 0.0)).astype(jnp.int32)
        home_rows = ((home_total + (BLOCK - 1)) // BLOCK) * BLOCK
        position = rank.astype(jnp.int32) + jnp.where(kind == 0, 0, home_rows)
        served = jnp.where(position < SERVE_BLOCKS * BLOCK, gates, 0.0)
        out_ref[q] = exact(in_ring, served).T


def load_kernel(*refs):
    count = len(refs) // 2
    copies = [pltpu.make_async_copy(refs[i], refs[count + i], refs[-1].at[i]) for i in range(count)]
    for copy in copies:
        copy.start()
    for copy in copies:
        copy.wait()


def load_call(*arrays):
    return pl.pallas_call(
        load_kernel,
        out_shape=[jax.ShapeDtypeStruct(x.shape, x.dtype) for x in arrays],
        in_specs=[pl.BlockSpec(memory_space=pl.ANY)] * len(arrays),
        out_specs=[pl.BlockSpec(memory_space=pltpu.VMEM)] * len(arrays),
        scratch_shapes=[pltpu.SemaphoreType.DMA((len(arrays),))],
        compiler_params=pltpu.CompilerParams(vmem_limit_bytes=16 * 2**20),
        cost_estimate=pl.CostEstimate(
            flops=0, bytes_accessed=sum(4 * x.size for x in arrays), transcendentals=0
        ),
    )(*arrays)


def expert_kernel(columns, gates_ref, *refs):
    refs = list(refs)
    x_all, hidden, total, x_sems = refs[-4:]
    halves = 2 * len(columns)
    x_refs, weights, out_refs = refs[:halves], refs[halves : halves + 4], refs[halves + 4 : -4]
    half = x_all.shape[0] // halves
    rows = 2 * half
    hidden_units, width = hidden.shape[1], x_all.shape[1]
    tile, step = hidden_units // 3, width // 4
    copies = [
        pltpu.make_async_copy(ref, x_all.at[pl.ds(i * half, half)], x_sems.at[i])
        for i, ref in enumerate(x_refs)
    ]
    for copy in copies:
        copy.start()
    for copy in copies:
        copy.wait()
    for q in range(2):
        in_ref, down_ref = weights[2 * q : 2 * q + 2]
        for f in range(0, hidden_units, tile):
            x = x_all[...]
            gate = jnp.dot(x, in_ref[0, :, f : f + tile], preferred_element_type=jnp.float32)
            up = jnp.dot(
                x,
                in_ref[0, :, hidden_units + f : hidden_units + f + tile],
                preferred_element_type=jnp.float32,
            )
            hidden[:, f : f + tile] = (gate / (1.0 + jnp.exp(-gate)) * up).astype(jnp.bfloat16)
        column = jnp.concatenate([gates_ref[q, :, d : d + 1] for d in columns])
        for n in range(0, width, step):
            out = jnp.dot(
                hidden[...], down_ref[0, :, n : n + step], preferred_element_type=jnp.float32
            )
            out = out.astype(jnp.bfloat16).astype(jnp.float32) * column
            if q == 0:
                total[:, n : n + step] = out
            else:
                out = (total[:, n : n + step] + out).astype(jnp.bfloat16)
                for i, ref in enumerate(out_refs):
                    ref[:, n : n + step] = out[i * half : (i + 1) * half]


def expert_call(halves, columns, gates, weights):
    half, width = halves[0].shape
    hidden_units = weights[1].shape[1]
    rows = half * len(halves)
    return pl.pallas_call(
        functools.partial(expert_kernel, columns),
        out_shape=[jax.ShapeDtypeStruct((half, width), jnp.bfloat16)] * len(halves),
        in_specs=[pl.BlockSpec(memory_space=pltpu.VMEM)]
        + [pl.BlockSpec(memory_space=pl.ANY)] * len(halves)
        + [pl.BlockSpec(memory_space=pltpu.VMEM)] * 4,
        out_specs=[pl.BlockSpec(memory_space=pltpu.VMEM)] * len(halves),
        scratch_shapes=[
            pltpu.VMEM((rows, width), jnp.bfloat16),
            pltpu.VMEM((rows, hidden_units), jnp.bfloat16),
            pltpu.VMEM((rows, width), jnp.float32),
            pltpu.SemaphoreType.DMA((len(halves),)),
        ],
        compiler_params=pltpu.CompilerParams(vmem_limit_bytes=16 * 2**20),
        cost_estimate=pl.CostEstimate(
            flops=2 * 2 * rows * width * 3 * hidden_units,
            bytes_accessed=2 * 2 * 3 * width * hidden_units,
            transcendentals=0,
        ),
    )(gates, *halves, *weights)


def gathered_body(tokens, expert_ids, route_gates, expert_in, expert_out, old_place, new_place):
    ep_size = lax.axis_size("ep")
    devices = ep_size * 2
    tok_rows = expert_ids.shape[0]
    half = tok_rows // 2
    reach = ep_size // 2
    ring = [*range(0, ep_size, 2), *range(ep_size - 1, 0, -2)]
    ahead = [(ring[i], ring[(i + 1) % ep_size]) for i in range(ep_size)]
    back = [(b, a) for a, b in ahead]
    ep = lax.axis_index("ep")
    own = ep * 2 + lax.axis_index("dp")

    def swap_cores(x):
        return lax.ppermute(x, "dp", [(0, 1), (1, 0)])

    def go(x, way):
        return lax.ppermute(x, "ep", ahead if way > 0 else back)

    def after(x, *others):
        return lax.optimization_barrier((x, *others))[0]

    vmem = pl.BlockSpec(memory_space=pltpu.VMEM)

    dense = pl.pallas_call(
        dense_kernel,
        out_shape=jax.ShapeDtypeStruct((1, devices, tok_rows), jnp.float32),
        in_specs=[vmem, vmem],
        out_specs=vmem,
    )(expert_ids.T, route_gates.T)

    def gather_gates(dense, step, *others):
        theirs = lax.ppermute(dense, "ep", [(i, i ^ (1 << step)) for i in range(ep_size)])
        return pl.pallas_call(
            join_kernel,
            out_shape=jax.ShapeDtypeStruct((2 << step, devices, tok_rows), jnp.float32),
            in_specs=[vmem, vmem],
            out_specs=vmem,
        )(after(dense, *others), theirs)

    weights = (expert_in, expert_out, swap_cores(expert_in), swap_cores(expert_out))
    held = {0: [tokens[:half], tokens[half:]]}

    def pass_on(d, *waits):
        held[-d] = [go(after(x, *w), 1) for x, w in zip(held[1 - d], waits)]
        held[d] = [go(after(x, *w), -1) for x, w in zip(held[d - 1], waits)]

    pass_on(1, [], [])
    for step in range(ep_size.bit_length() - 1):
        at = min(step + 1, reach - 1)
        if step + 1 < reach - 1:
            pass_on(step + 2, [], [])
        dense = gather_gates(dense, step, held[-at][1], held[at][1])
    held[reach] = [go(held[1 - reach][0], 1), go(held[reach - 1][1], -1)]
    weights = (*weights[:2], *load_call(*[after(w, dense) for w in weights[2:]]))
    gates = pl.pallas_call(
        gate_kernel,
        out_shape=jax.ShapeDtypeStruct((2, tok_rows, ep_size), jnp.float32),
        in_specs=[pl.BlockSpec(memory_space=pltpu.SMEM)] * 3 + [vmem] * 2,
        out_specs=vmem,
    )(own.reshape(1), old_place, new_place, dense, swap_cores(dense))

    part = {}

    def compute(distances, *waits):
        halves = [x for d in distances for x in held[d]]
        outs = expert_call(
            [after(halves[0], *waits), *halves[1:]],
            [d % ep_size for d in distances],
            gates,
            weights,
        )
        for i, d in enumerate(distances):
            part[d] = outs[2 * i : 2 * i + 2]
        return outs[0]

    def add(*xs):
        return sum(x.astype(jnp.float32) for x in xs).astype(jnp.bfloat16)

    compute([1 - reach, reach - 1])
    compute([reach])
    far, near = {1: 0, -1: 1}, {1: 1, -1: 0}
    moving = {way: part[reach][far[way]] for way in (1, -1)}
    late = {}
    for d in range(reach - 1, 0, -1):
        compute([1 - d, d - 1] if d > 1 else [0], *moving.values())
        moving = {way: go(x, way) for way, x in moving.items()}
        late = {
            way: go(add(*([late[way]] if late else []), part[way * d][near[way]]), way)
            for way in (1, -1)
        }
        first = part[1 - d][0]
        moving = {
            way: add(after(moving[way], first), part[way * d][far[way]]) for way in (1, -1)
        }
    moving = {way: go(x, way) for way, x in moving.items()}
    return jnp.concatenate(
        [add(part[0][0], moving[1], late[-1]), add(part[0][1], moving[-1], late[1])]
    )


def solution(mesh):
    placed = (
        P(("grp", "ep", "dp"), None),
        P(("grp", "ep", "dp"), None),
        P(("grp", "ep", "dp"), None),
        P(("grp", "ep", "dp"), None, None),
        P(("grp", "ep", "dp"), None, None),
        P(),
        P(),
    )

    def body(tokens, expert_ids, *rest):
        devices = lax.axis_size("ep") * lax.axis_size("dp")
        gathered = devices <= 2 * expert_ids.shape[1]
        return (gathered_body if gathered else routed_body)(tokens, expert_ids, *rest)

    return jax.shard_map(
        body, mesh=mesh, in_specs=placed, out_specs=P(("grp", "ep", "dp"), None), check_vma=False
    )
```

```python
import functools

import jax
import jax.numpy as jnp
from jax import lax
from jax.experimental import pallas as pl
from jax.experimental.pallas import tpu as pltpu
from jax.sharding import PartitionSpec as P

BLOCK = 128
SERVE_BLOCKS = 9


def expert_block(inputs, in_weights, out_weights, hidden_units):
    projected = jnp.dot(inputs, in_weights, preferred_element_type=jnp.float32)
    gate_part = projected[:, :hidden_units]
    up_part = projected[:, hidden_units:]
    hidden = (jax.nn.silu(gate_part) * up_part).astype(jnp.bfloat16)
    return jnp.dot(hidden, out_weights, preferred_element_type=jnp.float32).astype(jnp.bfloat16)


def routed_body(tokens, expert_ids, route_gates, expert_in, expert_out, old_place, new_place):
    ep_size = lax.axis_size("ep")
    dp_size = lax.axis_size("dp")
    devices = ep_size * dp_size
    tok_rows, top_count = expert_ids.shape
    model_width = tokens.shape[1]
    hidden_units = expert_out.shape[1]
    assigns = tok_rows * top_count
    capacity = (5 * assigns + 4 * devices - 1) // (4 * devices)
    serve_rows = SERVE_BLOCKS * BLOCK
    experts = jnp.arange(devices, dtype=jnp.int32)
    flat_ids = expert_ids.reshape(assigns)
    server = jnp.sum(
        jnp.where(flat_ids[:, None] == experts[None, :], old_place[None, :], 0), axis=1
    )
    onehot = (server[:, None] == experts[None, :]).astype(jnp.int32)
    local_rank = jnp.sum((jnp.cumsum(onehot, axis=0) - onehot) * onehot, axis=1)
    counts = jnp.sum(onehot, axis=0)
    slot_index = server * capacity + local_rank
    holder = (
        jnp.full((devices * capacity,), assigns, jnp.int32)
        .at[slot_index]
        .set(jnp.arange(assigns, dtype=jnp.int32))
    )
    token_index = jnp.where(holder < assigns, holder // top_count, tok_rows)
    send_rows = jnp.take(tokens, token_index, axis=0, mode="fill", fill_value=0).reshape(
        devices, capacity, model_width
    )
    recv_rows, recv_counts = (
        lax.all_to_all(send_rows, ("ep", "dp"), split_axis=0, concat_axis=0, tiled=True),
        lax.all_to_all(counts, ("ep", "dp"), split_axis=0, concat_axis=0, tiled=True),
    )
    source_home = experts % dp_size == 0
    home_counts = jnp.where(source_home, recv_counts, 0)
    rep_counts = recv_counts - home_counts
    earlier = jnp.where(
        source_home, jnp.cumsum(home_counts) - home_counts, jnp.cumsum(rep_counts) - rep_counts
    )
    home_blocks = (jnp.sum(home_counts) + BLOCK - 1) // BLOCK
    column = jnp.arange(capacity, dtype=jnp.int32)
    slot_rank = earlier[:, None] + column[None, :]
    present = column[None, :] < recv_counts[:, None]
    own_in = expert_in[0]
    own_out = expert_out[0]
    own_index = lax.axis_index("ep") * dp_size + lax.axis_index("dp")
    held_expert = jnp.sum(jnp.where(old_place == own_index, experts, 0))
    replica_server = jnp.sum(jnp.where(experts == held_expert, new_place, 0))
    all_blocks = lax.all_gather(
        home_blocks.astype(jnp.int32).reshape(1), ("ep", "dp"), axis=0, tiled=True
    )
    replica_blocks = jnp.sum(jnp.where(experts == replica_server, all_blocks, 0))
    base_rows = jnp.minimum(home_blocks, SERVE_BLOCKS) * BLOCK
    served_here = jnp.where(
        source_home[:, None],
        slot_rank < serve_rows,
        replica_blocks * BLOCK + slot_rank < serve_rows,
    )
    live_rows = present & served_here
    pack_rows = 2 * serve_rows
    position = jnp.where(source_home[:, None], slot_rank, base_rows + slot_rank)
    position = jnp.where(live_rows, position, pack_rows).reshape(devices * capacity)
    used_blocks = (jnp.max(jnp.where(position < pack_rows, position + 1, 0)) + BLOCK - 1) // BLOCK
    source_of = (
        jnp.full((pack_rows,), devices * capacity, jnp.int32)
        .at[position]
        .set(jnp.arange(devices * capacity, dtype=jnp.int32), mode="drop")
    )
    packed = jnp.take(
        recv_rows.reshape(devices * capacity, model_width),
        source_of,
        axis=0,
        mode="fill",
        fill_value=0,
    )

    def owner_block(state, block_id):
        inputs = lax.dynamic_slice_in_dim(packed, block_id * BLOCK, BLOCK, 0)
        result = lax.cond(
            block_id < used_blocks,
            lambda rows: expert_block(rows, own_in, own_out, hidden_units),
            lambda rows: jnp.zeros((BLOCK, model_width), jnp.bfloat16),
            inputs,
        )
        return (state, result)

    unused_state, outputs = lax.scan(
        owner_block, jnp.int32(0), jnp.arange(2 * SERVE_BLOCKS, dtype=jnp.int32)
    )
    results = jnp.take(
        outputs.reshape(pack_rows, model_width), position, axis=0, mode="fill", fill_value=0
    ).reshape(devices, capacity, model_width)
    returned = lax.all_to_all(results, ("ep", "dp"), split_axis=0, concat_axis=0, tiled=True)
    picked_rows = jnp.take(returned.reshape(devices * capacity, model_width), slot_index, axis=0)
    weighted = picked_rows.astype(jnp.float32) * route_gates.reshape(assigns)[:, None]
    return jnp.sum(weighted.reshape(tok_rows, top_count, model_width), axis=1).astype(jnp.bfloat16)


LANES = 128


def pack_kernel(experts, ids_ref, gates_ref, mate_ref, tokens_ref, out_ref, second_ref, copied):
    half, width = out_ref.shape[0], tokens_ref.shape[1]
    copies = [
        pltpu.make_async_copy(
            tokens_ref.at[pl.ds(0, half)], out_ref.at[:, pl.ds(0, width)], copied.at[0]
        ),
        pltpu.make_async_copy(tokens_ref.at[pl.ds(half, half)], second_ref, copied.at[1]),
    ]
    for copy in copies:
        copy.start()
    lane = lax.broadcasted_iota(jnp.int32, (2 * half, LANES), 1)
    expert = (lane % experts).astype(jnp.float32)
    ids, gates, mate = (
        ref[...].astype(jnp.float32).T for ref in (ids_ref, gates_ref, mate_ref)
    )
    dense = jnp.zeros((2 * half, LANES), jnp.float32)
    named = jnp.zeros((2 * half, LANES), jnp.float32)
    for k in range(ids.shape[1]):
        dense += jnp.where(ids[:, k : k + 1] == expert, gates[:, k : k + 1], 0.0)
        named += jnp.where(mate[:, k : k + 1] == expert, 1.0, 0.0)
    lane = lane[:half]
    dense = jnp.where(lane < 3 * experts, dense[:half], dense[half:])
    high = dense.astype(jnp.bfloat16).astype(jnp.float32)
    middle = (dense - high).astype(jnp.bfloat16).astype(jnp.float32)
    piece = lane // experts % 3
    packed = jnp.where(piece == 0, high, jnp.where(piece == 1, middle, dense - high - middle))
    totals = jnp.sum(named, axis=0, keepdims=True)
    packed = jnp.where(lane < 6 * experts, packed, jnp.where(lane < 7 * experts, totals, 0.0))
    out_ref[:, width:] = packed.astype(jnp.bfloat16)
    for copy in copies:
        copy.wait()


def served_gates(info_ref, old_ref, new_ref, packs):
    count, half = len(packs), packs[0].shape[0]
    experts = old_ref.shape[0]
    own = info_ref[0]
    kind, ep = own % 2, own // 2
    row = lax.broadcasted_iota(jnp.int32, (LANES, LANES), 0)
    col = lax.broadcasted_iota(jnp.int32, (LANES, LANES), 1)

    def at_expert(table, index):
        found = jnp.zeros(index.shape, jnp.int32)
        for e in range(experts):
            found = jnp.where(index == e, table[e], found)
        return found

    col_q, col_h, col_d = col // (2 * count), col // count % 2, col % count
    wanted = (
        (col < 4 * count)
        & (row < 6 * experts)
        & (row // (3 * experts) == col_h)
        & (at_expert(old_ref, row % experts) == (own ^ col_q))
    )
    place = jnp.where(ep % 2 == 0, ep // 2, count - (ep + 1) // 2)

    def source(d):
        turn = (place + d) % count
        return jnp.where(2 * turn < count, 2 * turn, 2 * (count - turn) - 1)

    row_q, row_h, row_d = row // (2 * count), row // count % 2, row % count
    first = source(row_d) * 2 + row_h
    second = source(col_d) * 2 + col_h
    before = (row < 4 * count) & (row_q == col_q) & (first < second)
    lane = lax.broadcasted_iota(jnp.int32, (8, LANES), 1)
    old, new = at_expert(old_ref, lane % experts), at_expert(new_ref, lane % experts)
    above = (
        lax.broadcasted_iota(jnp.int32, (half, half), 1)
        < lax.broadcasted_iota(jnp.int32, (half, half), 0)
    )

    def product(a, b):
        return jnp.dot(
            a.astype(jnp.bfloat16), b.astype(jnp.bfloat16), preferred_element_type=jnp.float32
        )

    def mask(x):
        return jnp.where(x, 1.0, 0.0)

    gates = jnp.zeros((half, LANES), jnp.float32)
    booked = jnp.zeros((8, LANES), jnp.float32)
    for d in range(count):
        gates += product(packs[d], mask(wanted & (col_d == d)))
        booked += packs[d][:8].astype(jnp.float32)
    chosen = mask(gates > 0.0)
    totals = jnp.broadcast_to(jnp.sum(chosen, axis=0, keepdims=True), (8, LANES))
    rank = product(mask(above), chosen) + product(totals, mask(before))[:1]
    home_rows = jnp.zeros((1, LANES), jnp.int32)
    for q in range(2):
        mine = (old == (own ^ q)) & (lane < experts)
        server = jnp.sum(jnp.where(mine, new, 0), axis=1, keepdims=True)
        theirs = (old == server) & (lane >= 6 * experts) & (lane < 7 * experts)
        home = jnp.sum(jnp.where(theirs, booked, 0.0), axis=1, keepdims=True)[:1].astype(jnp.int32)
        padded = ((home + (BLOCK - 1)) // BLOCK) * BLOCK
        home_rows = jnp.where(col_q[:1] == q, padded, home_rows)
    position = rank.astype(jnp.int32) + jnp.where(kind == 0, 0, home_rows)
    return jnp.where(position < SERVE_BLOCKS * BLOCK, gates, 0.0)


def load_kernel(places, in_ref, down_ref, *refs):
    *blocks, in_out, down_out, packs, sems = refs
    width = blocks[0].shape[1] - LANES
    copies = [
        pltpu.make_async_copy(ref.at[:, pl.ds(width, LANES)], packs.at[d], sems.at[i])
        for i, (d, ref) in enumerate(zip(places, blocks))
    ]
    copies.append(pltpu.make_async_copy(in_ref, in_out, sems.at[len(blocks)]))
    copies.append(pltpu.make_async_copy(down_ref, down_out, sems.at[len(blocks) + 1]))
    for copy in copies:
        copy.start()
    for copy in copies:
        copy.wait()


def load_call(weights, blocks):
    half, dtype = blocks[0].shape[0], blocks[0].dtype
    return pl.pallas_call(
        functools.partial(load_kernel, tuple(blocks)),
        out_shape=[jax.ShapeDtypeStruct(x.shape, x.dtype) for x in weights]
        + [jax.ShapeDtypeStruct((len(blocks) + 1, half, LANES), dtype)],
        in_specs=[pl.BlockSpec(memory_space=pl.ANY)] * (2 + len(blocks)),
        out_specs=[pl.BlockSpec(memory_space=pltpu.VMEM)] * 3,
        scratch_shapes=[pltpu.SemaphoreType.DMA((2 + len(blocks),))],
        compiler_params=pltpu.CompilerParams(vmem_limit_bytes=16 * 2**20),
        cost_estimate=pl.CostEstimate(
            flops=0, bytes_accessed=sum(4 * x.size for x in weights), transcendentals=0
        ),
    )(*weights, *blocks.values())


def gate_lanes(q, column):
    block, count = column
    return [(2 * q + h) * count + block for h in range(2)]


def expert_kernel(blocks, columns, first, *refs):
    refs = list(refs)
    halves = 2 * blocks
    if first:
        info_ref, old_ref, new_ref, packs_ref, *refs = refs
        gates_ref, pack, pack_sem = refs.pop(halves + 4), *refs[-2:]
        refs = refs[:-2]
        pack_copy = pltpu.make_async_copy(
            refs[0].at[:, pl.ds(refs[1].shape[1], LANES)], pack, pack_sem
        )
        pack_copy.start()
    elif columns:
        gates_ref, *refs = refs
    x_all, hidden, total, x_sems = refs[-4:]
    x_refs, weights, out_refs = refs[:halves], refs[halves : halves + 4], refs[halves + 4 : -4]
    half = x_all.shape[0] // halves
    rows = 2 * half
    hidden_units, width = hidden.shape[1], x_all.shape[1]
    tile, step = hidden_units // 3, width // 4
    copies = [
        pltpu.make_async_copy(
            ref.at[:, pl.ds(0, x_all.shape[1])], x_all.at[pl.ds(i * half, half)], x_sems.at[i]
        )
        for i, ref in enumerate(x_refs)
    ]
    for copy in copies:
        copy.start()
    if first:
        pack_copy.wait()
        at = columns[0][0]
        gates_ref[...] = served_gates(
            info_ref,
            old_ref,
            new_ref,
            [pack[...] if d == at else packs_ref[d] for d in range(packs_ref.shape[0])],
        )
    for copy in copies:
        copy.wait()
    for q in range(2):
        in_ref, down_ref = weights[2 * q : 2 * q + 2]
        for f in range(0, hidden_units, tile):
            x = x_all[...]
            gate = jnp.dot(x, in_ref[0, :, f : f + tile], preferred_element_type=jnp.float32)
            up = jnp.dot(
                x,
                in_ref[0, :, hidden_units + f : hidden_units + f + tile],
                preferred_element_type=jnp.float32,
            )
            hidden[:, f : f + tile] = (gate / (1.0 + jnp.exp(-gate)) * up).astype(jnp.bfloat16)
        if columns:
            column = jnp.concatenate(
                [gates_ref[:, at : at + 1] for d in columns for at in gate_lanes(q, d)]
            )
        for n in range(0, width, step):
            out = jnp.dot(
                hidden[...], down_ref[0, :, n : n + step], preferred_element_type=jnp.float32
            )
            out = out.astype(jnp.bfloat16)
            if not columns:
                for i in range(blocks):
                    out_refs[q * blocks + i][:, n : n + step] = out[i * rows : (i + 1) * rows]
                continue
            out = out.astype(jnp.float32) * column
            if q == 0:
                total[:, n : n + step] = out
            else:
                out = (total[:, n : n + step] + out).astype(jnp.bfloat16)
                for i, ref in enumerate(out_refs):
                    ref[:, n : n + step] = out[i * half : (i + 1) * half]


def expert_call(halves, weights, columns=(), gates=(), tables=()):
    half, width = halves[1].shape
    hidden_units = weights[1].shape[1]
    blocks = len(halves) // 2
    rows = half * len(halves)
    vmem = pl.BlockSpec(memory_space=pltpu.VMEM)
    out = jax.ShapeDtypeStruct((half if columns else 2 * half, width), jnp.bfloat16)
    made = [jax.ShapeDtypeStruct((half, LANES), jnp.float32)] if tables else []
    return pl.pallas_call(
        functools.partial(expert_kernel, blocks, columns, bool(tables)),
        out_shape=made + [out] * len(halves),
        in_specs=([pl.BlockSpec(memory_space=pltpu.SMEM)] * 3 + [vmem] if tables else [])
        + [vmem] * len(gates)
        + [pl.BlockSpec(memory_space=pl.ANY)] * len(halves)
        + [vmem] * 4,
        out_specs=[vmem] * (len(made) + len(halves)),
        scratch_shapes=[
            pltpu.VMEM((rows, width), jnp.bfloat16),
            pltpu.VMEM((rows, hidden_units), jnp.bfloat16),
            pltpu.VMEM((rows, width), jnp.float32),
            pltpu.SemaphoreType.DMA((len(halves),)),
        ]
        + ([pltpu.VMEM((half, LANES), jnp.bfloat16), pltpu.SemaphoreType.DMA] if tables else []),
        compiler_params=pltpu.CompilerParams(vmem_limit_bytes=16 * 2**20),
        cost_estimate=pl.CostEstimate(
            flops=2 * 2 * rows * width * 3 * hidden_units,
            bytes_accessed=2 * 2 * 3 * width * hidden_units,
            transcendentals=0,
        ),
    )(*tables, *gates, *halves, *weights)


def sum_kernel(spec, gates_ref, *refs):
    refs = list(refs)
    outs = refs[len(refs) - len(spec) :]
    for at, (d, h, came) in enumerate(spec):
        so_far, refs = refs[:came], refs[came:]
        made, refs = refs[:2], refs[2:]
        rows = slice(h * outs[at].shape[0], (h + 1) * outs[at].shape[0])
        total = None
        for q in range(2):
            lane = gate_lanes(q, d)[h]
            term = made[q][rows, :].astype(jnp.float32) * gates_ref[:, lane : lane + 1]
            total = term if total is None else total + term
        for ref in so_far:
            total = total + ref[...].astype(jnp.float32)
        outs[at][...] = total.astype(jnp.bfloat16)


def sum_call(gates, items):
    half, width = items[0][3][0].shape[0] // 2, items[0][3][0].shape[1]
    spec = [(d, h, len(came)) for d, h, came, _ in items]
    arrays = [x for _, _, came, made in items for x in [*came, *made]]
    return pl.pallas_call(
        functools.partial(sum_kernel, spec),
        out_shape=[jax.ShapeDtypeStruct((half, width), jnp.bfloat16)] * len(items),
        in_specs=[pl.BlockSpec(memory_space=pltpu.VMEM)] * (1 + len(arrays)),
        out_specs=[pl.BlockSpec(memory_space=pltpu.VMEM)] * len(items),
        compiler_params=pltpu.CompilerParams(vmem_limit_bytes=16 * 2**20),
        cost_estimate=pl.CostEstimate(
            flops=0, bytes_accessed=8 * half * width * len(items), transcendentals=0
        ),
    )(gates, *arrays)


def gathered_body(tokens, expert_ids, route_gates, expert_in, expert_out, old_place, new_place):
    ep_size = lax.axis_size("ep")
    devices = ep_size * 2
    tok_rows = expert_ids.shape[0]
    half = tok_rows // 2
    reach = ep_size // 2
    ring = [*range(0, ep_size, 2), *range(ep_size - 1, 0, -2)]
    ahead = [(ring[i], ring[(i + 1) % ep_size]) for i in range(ep_size)]
    back = [(b, a) for a, b in ahead]
    ep = lax.axis_index("ep")
    own = ep * 2 + lax.axis_index("dp")

    def swap_cores(x):
        return lax.ppermute(x, "dp", [(0, 1), (1, 0)])

    def go(x, way):
        return lax.ppermute(x, "ep", ahead if way > 0 else back)

    def after(x, *others):
        return lax.optimization_barrier((x, *others))[0]

    vmem = pl.BlockSpec(memory_space=pltpu.VMEM)

    ids, any_space = expert_ids.T, pl.BlockSpec(memory_space=pl.ANY)
    packed, second = pl.pallas_call(
        functools.partial(pack_kernel, devices),
        out_shape=[
            jax.ShapeDtypeStruct((half, tokens.shape[1] + extra), tokens.dtype)
            for extra in (LANES, 0)
        ],
        in_specs=[vmem] * 3 + [any_space],
        out_specs=[vmem] * 2,
        scratch_shapes=[pltpu.SemaphoreType.DMA((2,))],
    )(ids, route_gates.T, swap_cores(ids), tokens)

    weights = (expert_in, expert_out, *[swap_cores(after(w, packed)) for w in (expert_in, expert_out)])
    held = {0: [packed, second]}

    def pass_on(d, *waits):
        held[-d] = [go(after(x, *w), 1) for x, w in zip(held[1 - d], waits)]
        held[d] = [go(after(x, *w), -1) for x, w in zip(held[d - 1], waits)]

    for d in range(1, reach):
        pass_on(d, [], [])
    last = reach - 1
    held[reach] = [go(held[-last][0], 1), go(held[last][1], -1)]
    come = [held[way * last][0] for way in (1, -1)]
    *loaded, packs = load_call(
        [after(w, *come) for w in weights[2:]],
        {d % ep_size: held[d][0] for d in range(-last, reach)},
    )
    weights = (*weights[:2], *loaded)
    apart = expert_call([x for d in (-last, last) for x in held[d]], weights)
    apart = {-last: apart[::2], last: apart[1::2]}
    gates, *outs = expert_call(
        held[reach],
        weights,
        ((reach, ep_size),),
        tables=(after(own.reshape(1), apart[last][0]), old_place, new_place, packs),
    )
    part = {reach: outs}

    def compute(distances, *waits):
        halves = [x for d in distances for x in held[d]]
        outs = expert_call(
            [after(halves[0], *waits), *halves[1:]],
            weights,
            tuple((d % ep_size, ep_size) for d in distances),
            (gates,),
        )
        for i, d in enumerate(distances):
            part[d] = outs[2 * i : 2 * i + 2]

    def gated(half_of, came):
        outs = sum_call(
            gates, [
                ((way * last % ep_size, ep_size), half_of[way], came[way], apart[way * last])
                for way in (1, -1)
            ],
        )
        return dict(zip((1, -1), outs))

    def add(*xs):
        return sum(x.astype(jnp.float32) for x in xs).astype(jnp.bfloat16)

    far, near = {1: 0, -1: 1}, {1: 1, -1: 0}
    moving = {way: part[reach][far[way]] for way in (1, -1)}
    late = gated(near, {1: [], -1: []})
    for d in range(last, 0, -1):
        if d < last:
            late = {way: add(late[way], part[way * d][near[way]]) for way in (1, -1)}
        compute([1 - d, d - 1] if d > 1 else [0], *moving.values())
        moving = {way: go(x, way) for way, x in moving.items()}
        late = {way: go(x, way) for way, x in late.items()}
        moving = {way: after(x, part[1 - d][0]) for way, x in moving.items()}
        if d == last:
            moving = gated(far, {way: [x] for way, x in moving.items()})
        else:
            moving = {way: add(x, part[way * d][far[way]]) for way, x in moving.items()}
    moving = {way: go(x, way) for way, x in moving.items()}
    return jnp.concatenate(
        [add(part[0][0], moving[1], late[-1]), add(part[0][1], moving[-1], late[1])]
    )


def solution(mesh):
    placed = (
        P(("grp", "ep", "dp"), None),
        P(("grp", "ep", "dp"), None),
        P(("grp", "ep", "dp"), None),
        P(("grp", "ep", "dp"), None, None),
        P(("grp", "ep", "dp"), None, None),
        P(),
        P(),
    )

    def body(tokens, expert_ids, *rest):
        devices = lax.axis_size("ep") * lax.axis_size("dp")
        gathered = devices <= 2 * expert_ids.shape[1] and 7 * devices <= LANES
        return (gathered_body if gathered else routed_body)(tokens, expert_ids, *rest)

    return jax.shard_map(
        body, mesh=mesh, in_specs=placed, out_specs=P(("grp", "ep", "dp"), None), check_vma=False
    )
```

```python
import functools

import jax
import jax.numpy as jnp
from jax import lax
from jax.experimental import pallas as pl
from jax.experimental.pallas import tpu as pltpu
from jax.sharding import PartitionSpec as P

BLOCK = 128
SERVE_BLOCKS = 9


def expert_block(inputs, in_weights, out_weights, hidden_units):
    projected = jnp.dot(inputs, in_weights, preferred_element_type=jnp.float32)
    gate_part = projected[:, :hidden_units]
    up_part = projected[:, hidden_units:]
    hidden = (jax.nn.silu(gate_part) * up_part).astype(jnp.bfloat16)
    return jnp.dot(hidden, out_weights, preferred_element_type=jnp.float32).astype(jnp.bfloat16)


def routed_body(tokens, expert_ids, route_gates, expert_in, expert_out, old_place, new_place):
    ep_size = lax.axis_size("ep")
    dp_size = lax.axis_size("dp")
    devices = ep_size * dp_size
    tok_rows, top_count = expert_ids.shape
    model_width = tokens.shape[1]
    hidden_units = expert_out.shape[1]
    assigns = tok_rows * top_count
    capacity = (5 * assigns + 4 * devices - 1) // (4 * devices)
    serve_rows = SERVE_BLOCKS * BLOCK
    experts = jnp.arange(devices, dtype=jnp.int32)
    flat_ids = expert_ids.reshape(assigns)
    server = jnp.sum(
        jnp.where(flat_ids[:, None] == experts[None, :], old_place[None, :], 0), axis=1
    )
    onehot = (server[:, None] == experts[None, :]).astype(jnp.int32)
    local_rank = jnp.sum((jnp.cumsum(onehot, axis=0) - onehot) * onehot, axis=1)
    counts = jnp.sum(onehot, axis=0)
    slot_index = server * capacity + local_rank
    holder = (
        jnp.full((devices * capacity,), assigns, jnp.int32)
        .at[slot_index]
        .set(jnp.arange(assigns, dtype=jnp.int32))
    )
    token_index = jnp.where(holder < assigns, holder // top_count, tok_rows)
    send_rows = jnp.take(tokens, token_index, axis=0, mode="fill", fill_value=0).reshape(
        devices, capacity, model_width
    )
    recv_rows, recv_counts = (
        lax.all_to_all(send_rows, ("ep", "dp"), split_axis=0, concat_axis=0, tiled=True),
        lax.all_to_all(counts, ("ep", "dp"), split_axis=0, concat_axis=0, tiled=True),
    )
    source_home = experts % dp_size == 0
    home_counts = jnp.where(source_home, recv_counts, 0)
    rep_counts = recv_counts - home_counts
    earlier = jnp.where(
        source_home, jnp.cumsum(home_counts) - home_counts, jnp.cumsum(rep_counts) - rep_counts
    )
    home_blocks = (jnp.sum(home_counts) + BLOCK - 1) // BLOCK
    column = jnp.arange(capacity, dtype=jnp.int32)
    slot_rank = earlier[:, None] + column[None, :]
    present = column[None, :] < recv_counts[:, None]
    own_in = expert_in[0]
    own_out = expert_out[0]
    own_index = lax.axis_index("ep") * dp_size + lax.axis_index("dp")
    held_expert = jnp.sum(jnp.where(old_place == own_index, experts, 0))
    replica_server = jnp.sum(jnp.where(experts == held_expert, new_place, 0))
    all_blocks = lax.all_gather(
        home_blocks.astype(jnp.int32).reshape(1), ("ep", "dp"), axis=0, tiled=True
    )
    replica_blocks = jnp.sum(jnp.where(experts == replica_server, all_blocks, 0))
    base_rows = jnp.minimum(home_blocks, SERVE_BLOCKS) * BLOCK
    served_here = jnp.where(
        source_home[:, None],
        slot_rank < serve_rows,
        replica_blocks * BLOCK + slot_rank < serve_rows,
    )
    live_rows = present & served_here
    pack_rows = 2 * serve_rows
    position = jnp.where(source_home[:, None], slot_rank, base_rows + slot_rank)
    position = jnp.where(live_rows, position, pack_rows).reshape(devices * capacity)
    used_blocks = (jnp.max(jnp.where(position < pack_rows, position + 1, 0)) + BLOCK - 1) // BLOCK
    source_of = (
        jnp.full((pack_rows,), devices * capacity, jnp.int32)
        .at[position]
        .set(jnp.arange(devices * capacity, dtype=jnp.int32), mode="drop")
    )
    packed = jnp.take(
        recv_rows.reshape(devices * capacity, model_width),
        source_of,
        axis=0,
        mode="fill",
        fill_value=0,
    )

    def owner_block(state, block_id):
        inputs = lax.dynamic_slice_in_dim(packed, block_id * BLOCK, BLOCK, 0)
        result = lax.cond(
            block_id < used_blocks,
            lambda rows: expert_block(rows, own_in, own_out, hidden_units),
            lambda rows: jnp.zeros((BLOCK, model_width), jnp.bfloat16),
            inputs,
        )
        return (state, result)

    unused_state, outputs = lax.scan(
        owner_block, jnp.int32(0), jnp.arange(2 * SERVE_BLOCKS, dtype=jnp.int32)
    )
    results = jnp.take(
        outputs.reshape(pack_rows, model_width), position, axis=0, mode="fill", fill_value=0
    ).reshape(devices, capacity, model_width)
    returned = lax.all_to_all(results, ("ep", "dp"), split_axis=0, concat_axis=0, tiled=True)
    picked_rows = jnp.take(returned.reshape(devices * capacity, model_width), slot_index, axis=0)
    weighted = picked_rows.astype(jnp.float32) * route_gates.reshape(assigns)[:, None]
    return jnp.sum(weighted.reshape(tok_rows, top_count, model_width), axis=1).astype(jnp.bfloat16)


LANES = 128


def pack_kernel(experts, ids_ref, gates_ref, mate_ref, tokens_ref, out_ref, second_ref, copied):
    half, width = out_ref.shape[0], tokens_ref.shape[1]
    copies = [
        pltpu.make_async_copy(
            tokens_ref.at[pl.ds(0, half)], out_ref.at[:, pl.ds(0, width)], copied.at[0]
        ),
        pltpu.make_async_copy(tokens_ref.at[pl.ds(half, half)], second_ref, copied.at[1]),
    ]
    for copy in copies:
        copy.start()
    lane = lax.broadcasted_iota(jnp.int32, (2 * half, LANES), 1)
    expert = (lane % experts).astype(jnp.float32)
    ids, gates, mate = (
        ref[...].astype(jnp.float32).T for ref in (ids_ref, gates_ref, mate_ref)
    )
    dense = jnp.zeros((2 * half, LANES), jnp.float32)
    named = jnp.zeros((2 * half, LANES), jnp.float32)
    for k in range(ids.shape[1]):
        dense += jnp.where(ids[:, k : k + 1] == expert, gates[:, k : k + 1], 0.0)
        named += jnp.where(mate[:, k : k + 1] == expert, 1.0, 0.0)
    lane = lane[:half]
    dense = jnp.where(lane < 3 * experts, dense[:half], dense[half:])
    high = dense.astype(jnp.bfloat16).astype(jnp.float32)
    middle = (dense - high).astype(jnp.bfloat16).astype(jnp.float32)
    piece = lane // experts % 3
    packed = jnp.where(piece == 0, high, jnp.where(piece == 1, middle, dense - high - middle))
    totals = jnp.sum(named, axis=0, keepdims=True)
    packed = jnp.where(lane < 6 * experts, packed, jnp.where(lane < 7 * experts, totals, 0.0))
    out_ref[:, width:] = packed.astype(jnp.bfloat16)
    for copy in copies:
        copy.wait()


def served_gates(info_ref, old_ref, new_ref, packs):
    count, half = len(packs), packs[0].shape[0]
    experts = old_ref.shape[0]
    own = info_ref[0]
    kind, ep = own % 2, own // 2
    row = lax.broadcasted_iota(jnp.int32, (LANES, LANES), 0)
    col = lax.broadcasted_iota(jnp.int32, (LANES, LANES), 1)

    def at_expert(table, index):
        found = jnp.zeros(index.shape, jnp.int32)
        for e in range(experts):
            found = jnp.where(index == e, table[e], found)
        return found

    col_q, col_h, col_d = col // (2 * count), col // count % 2, col % count
    wanted = (
        (col < 4 * count)
        & (row < 6 * experts)
        & (row // (3 * experts) == col_h)
        & (at_expert(old_ref, row % experts) == (own ^ col_q))
    )
    place = jnp.where(ep % 2 == 0, ep // 2, count - (ep + 1) // 2)

    def source(d):
        turn = (place + d) % count
        return jnp.where(2 * turn < count, 2 * turn, 2 * (count - turn) - 1)

    row_q, row_h, row_d = row // (2 * count), row // count % 2, row % count
    first = source(row_d) * 2 + row_h
    second = source(col_d) * 2 + col_h
    before = (row < 4 * count) & (row_q == col_q) & (first < second)
    lane = lax.broadcasted_iota(jnp.int32, (8, LANES), 1)
    old, new = at_expert(old_ref, lane % experts), at_expert(new_ref, lane % experts)
    above = (
        lax.broadcasted_iota(jnp.int32, (half, half), 1)
        < lax.broadcasted_iota(jnp.int32, (half, half), 0)
    )

    def product(a, b):
        return jnp.dot(
            a.astype(jnp.bfloat16), b.astype(jnp.bfloat16), preferred_element_type=jnp.float32
        )

    def mask(x):
        return jnp.where(x, 1.0, 0.0)

    gates = jnp.zeros((half, LANES), jnp.float32)
    booked = jnp.zeros((8, LANES), jnp.float32)
    for d in range(count):
        gates += product(packs[d], mask(wanted & (col_d == d)))
        booked += packs[d][:8].astype(jnp.float32)
    chosen = mask(gates > 0.0)
    totals = jnp.broadcast_to(jnp.sum(chosen, axis=0, keepdims=True), (8, LANES))
    rank = product(mask(above), chosen) + product(totals, mask(before))[:1]
    home_rows = jnp.zeros((1, LANES), jnp.int32)
    for q in range(2):
        mine = (old == (own ^ q)) & (lane < experts)
        server = jnp.sum(jnp.where(mine, new, 0), axis=1, keepdims=True)
        theirs = (old == server) & (lane >= 6 * experts) & (lane < 7 * experts)
        home = jnp.sum(jnp.where(theirs, booked, 0.0), axis=1, keepdims=True)[:1].astype(jnp.int32)
        padded = ((home + (BLOCK - 1)) // BLOCK) * BLOCK
        home_rows = jnp.where(col_q[:1] == q, padded, home_rows)
    position = rank.astype(jnp.int32) + jnp.where(kind == 0, 0, home_rows)
    return jnp.where(position < SERVE_BLOCKS * BLOCK, gates, 0.0)


def load_kernel(places, in_ref, down_ref, *refs):
    *blocks, in_out, down_out, packs, sems = refs
    width = blocks[0].shape[1] - LANES
    copies = [
        pltpu.make_async_copy(ref.at[:, pl.ds(width, LANES)], packs.at[d], sems.at[i])
        for i, (d, ref) in enumerate(zip(places, blocks))
    ]
    copies.append(pltpu.make_async_copy(in_ref, in_out, sems.at[len(blocks)]))
    copies.append(pltpu.make_async_copy(down_ref, down_out, sems.at[len(blocks) + 1]))
    for copy in copies:
        copy.start()
    for copy in copies:
        copy.wait()


def load_call(weights, blocks):
    half, dtype = blocks[0].shape[0], blocks[0].dtype
    return pl.pallas_call(
        functools.partial(load_kernel, tuple(blocks)),
        out_shape=[jax.ShapeDtypeStruct(x.shape, x.dtype) for x in weights]
        + [jax.ShapeDtypeStruct((len(blocks) + 1, half, LANES), dtype)],
        in_specs=[pl.BlockSpec(memory_space=pl.ANY)] * (2 + len(blocks)),
        out_specs=[pl.BlockSpec(memory_space=pltpu.VMEM)] * 3,
        scratch_shapes=[pltpu.SemaphoreType.DMA((2 + len(blocks),))],
        compiler_params=pltpu.CompilerParams(vmem_limit_bytes=16 * 2**20),
        cost_estimate=pl.CostEstimate(
            flops=0, bytes_accessed=sum(4 * x.size for x in weights), transcendentals=0
        ),
    )(*weights, *blocks.values())


def gate_lanes(q, column):
    block, count = column
    return [(2 * q + h) * count + block for h in range(2)]


def expert_kernel(blocks, columns, first, *refs):
    refs = list(refs)
    halves = 2 * blocks
    if first:
        info_ref, old_ref, new_ref, packs_ref, *refs = refs
        gates_ref, pack, pack_sem = refs.pop(halves + 4), *refs[-2:]
        refs = refs[:-2]
        pack_copy = pltpu.make_async_copy(
            refs[0].at[:, pl.ds(refs[1].shape[1], LANES)], pack, pack_sem
        )
        pack_copy.start()
    elif columns:
        gates_ref, *refs = refs
    x_all, hidden, total, x_sems = refs[-4:]
    x_refs, weights, out_refs = refs[:halves], refs[halves : halves + 4], refs[halves + 4 : -4]
    half = x_all.shape[0] // halves
    rows = 2 * half
    hidden_units, width = hidden.shape[1], x_all.shape[1]
    tile, step = hidden_units // 3, width // 4
    copies = [
        pltpu.make_async_copy(
            ref.at[:, pl.ds(0, x_all.shape[1])], x_all.at[pl.ds(i * half, half)], x_sems.at[i]
        )
        for i, ref in enumerate(x_refs)
    ]
    for copy in copies:
        copy.start()
    if first:
        pack_copy.wait()
        at = columns[0][0]
        gates_ref[...] = served_gates(
            info_ref,
            old_ref,
            new_ref,
            [pack[...] if d == at else packs_ref[d] for d in range(packs_ref.shape[0])],
        )
    for copy in copies:
        copy.wait()
    for q in range(2):
        in_ref, down_ref = weights[2 * q : 2 * q + 2]
        for f in range(0, hidden_units, tile):
            x = x_all[...]
            gate = jnp.dot(x, in_ref[0, :, f : f + tile], preferred_element_type=jnp.float32)
            up = jnp.dot(
                x,
                in_ref[0, :, hidden_units + f : hidden_units + f + tile],
                preferred_element_type=jnp.float32,
            )
            hidden[:, f : f + tile] = (gate / (1.0 + jnp.exp(-gate)) * up).astype(jnp.bfloat16)
        if columns:
            column = jnp.concatenate(
                [gates_ref[:, at : at + 1] for d in columns for at in gate_lanes(q, d)]
            )
        for n in range(0, width, step):
            out = jnp.dot(
                hidden[...], down_ref[0, :, n : n + step], preferred_element_type=jnp.float32
            )
            out = out.astype(jnp.bfloat16)
            if not columns:
                for i in range(blocks):
                    out_refs[q * blocks + i][:, n : n + step] = out[i * rows : (i + 1) * rows]
                continue
            out = out.astype(jnp.float32) * column
            if q == 0:
                total[:, n : n + step] = out
            else:
                out = (total[:, n : n + step] + out).astype(jnp.bfloat16)
                for i, ref in enumerate(out_refs):
                    ref[:, n : n + step] = out[i * half : (i + 1) * half]


def expert_call(halves, weights, columns=(), gates=(), tables=()):
    half, width = halves[1].shape
    hidden_units = weights[1].shape[1]
    blocks = len(halves) // 2
    rows = half * len(halves)
    vmem = pl.BlockSpec(memory_space=pltpu.VMEM)
    out = jax.ShapeDtypeStruct((half if columns else 2 * half, width), jnp.bfloat16)
    made = [jax.ShapeDtypeStruct((half, LANES), jnp.float32)] if tables else []
    return pl.pallas_call(
        functools.partial(expert_kernel, blocks, columns, bool(tables)),
        out_shape=made + [out] * len(halves),
        in_specs=([pl.BlockSpec(memory_space=pltpu.SMEM)] * 3 + [vmem] if tables else [])
        + [vmem] * len(gates)
        + [pl.BlockSpec(memory_space=pl.ANY)] * len(halves)
        + [vmem] * 4,
        out_specs=[vmem] * (len(made) + len(halves)),
        scratch_shapes=[
            pltpu.VMEM((rows, width), jnp.bfloat16),
            pltpu.VMEM((rows, hidden_units), jnp.bfloat16),
            pltpu.VMEM((rows, width), jnp.float32),
            pltpu.SemaphoreType.DMA((len(halves),)),
        ]
        + ([pltpu.VMEM((half, LANES), jnp.bfloat16), pltpu.SemaphoreType.DMA] if tables else []),
        compiler_params=pltpu.CompilerParams(vmem_limit_bytes=16 * 2**20),
        cost_estimate=pl.CostEstimate(
            flops=2 * 2 * rows * width * 3 * hidden_units,
            bytes_accessed=2 * 2 * 3 * width * hidden_units,
            transcendentals=0,
        ),
    )(*tables, *gates, *halves, *weights)


def sum_kernel(spec, gates_ref, *refs):
    refs = list(refs)
    outs = refs[len(refs) - len(spec) :]
    for at, (d, h, came) in enumerate(spec):
        so_far, refs = refs[:came], refs[came:]
        made, refs = refs[:2], refs[2:]
        rows = slice(h * outs[at].shape[0], (h + 1) * outs[at].shape[0])
        total = None
        for q in range(2):
            lane = gate_lanes(q, d)[h]
            term = made[q][rows, :].astype(jnp.float32) * gates_ref[:, lane : lane + 1]
            total = term if total is None else total + term
        for ref in so_far:
            total = total + ref[...].astype(jnp.float32)
        outs[at][...] = total.astype(jnp.bfloat16)


def sum_call(gates, items):
    half, width = items[0][3][0].shape[0] // 2, items[0][3][0].shape[1]
    spec = [(d, h, len(came)) for d, h, came, _ in items]
    arrays = [x for _, _, came, made in items for x in [*came, *made]]
    return pl.pallas_call(
        functools.partial(sum_kernel, spec),
        out_shape=[jax.ShapeDtypeStruct((half, width), jnp.bfloat16)] * len(items),
        in_specs=[pl.BlockSpec(memory_space=pltpu.VMEM)] * (1 + len(arrays)),
        out_specs=[pl.BlockSpec(memory_space=pltpu.VMEM)] * len(items),
        compiler_params=pltpu.CompilerParams(vmem_limit_bytes=16 * 2**20),
        cost_estimate=pl.CostEstimate(
            flops=0, bytes_accessed=8 * half * width * len(items), transcendentals=0
        ),
    )(gates, *arrays)


def gathered_body(tokens, expert_ids, route_gates, expert_in, expert_out, old_place, new_place):
    ep_size = lax.axis_size("ep")
    devices = ep_size * 2
    tok_rows = expert_ids.shape[0]
    half = tok_rows // 2
    reach = ep_size // 2
    ring = [*range(0, ep_size, 2), *range(ep_size - 1, 0, -2)]
    ahead = [(ring[i], ring[(i + 1) % ep_size]) for i in range(ep_size)]
    back = [(b, a) for a, b in ahead]
    ep = lax.axis_index("ep")
    own = ep * 2 + lax.axis_index("dp")

    def swap_cores(x):
        return lax.ppermute(x, "dp", [(0, 1), (1, 0)])

    def go(x, way):
        return lax.ppermute(x, "ep", ahead if way > 0 else back)

    def after(x, *others):
        return lax.optimization_barrier((x, *others))[0]

    vmem = pl.BlockSpec(memory_space=pltpu.VMEM)

    ids, any_space = expert_ids.T, pl.BlockSpec(memory_space=pl.ANY)
    packed, second = pl.pallas_call(
        functools.partial(pack_kernel, devices),
        out_shape=[
            jax.ShapeDtypeStruct((half, tokens.shape[1] + extra), tokens.dtype)
            for extra in (LANES, 0)
        ],
        in_specs=[vmem] * 3 + [any_space],
        out_specs=[vmem] * 2,
        scratch_shapes=[pltpu.SemaphoreType.DMA((2,))],
    )(ids, route_gates.T, swap_cores(ids), tokens)

    weights = (expert_in, expert_out, *[swap_cores(after(w, packed)) for w in (expert_in, expert_out)])
    held = {0: [packed, second]}

    def pass_on(d, *waits):
        held[-d] = [go(after(x, *w), 1) for x, w in zip(held[1 - d], waits)]
        held[d] = [go(after(x, *w), -1) for x, w in zip(held[d - 1], waits)]

    last = reach - 1
    for d in range(1, reach):
        if d == last:
            for way in (1, -1):
                held[way * (d - 1)][1] = after(held[way * (d - 1)][1], *weights[2:])
        pass_on(d, [], [])
    held[reach] = [go(held[-last][0], 1), go(held[last][1], -1)]
    come = [held[way * last][0] for way in (1, -1)]
    *loaded, packs = load_call(
        [after(w, *come) for w in weights[2:]],
        {d % ep_size: held[d][0] for d in range(-last, reach)},
    )
    weights = (*weights[:2], *loaded)
    apart = expert_call([x for d in (-last, last) for x in held[d]], weights)
    apart = {-last: apart[::2], last: apart[1::2]}
    gates, *outs = expert_call(
        held[reach],
        weights,
        ((reach, ep_size),),
        tables=(after(own.reshape(1), apart[last][0]), old_place, new_place, packs),
    )
    part = {reach: outs}

    def compute(distances, *waits):
        halves = [x for d in distances for x in held[d]]
        outs = expert_call(
            [after(halves[0], *waits), *halves[1:]],
            weights,
            tuple((d % ep_size, ep_size) for d in distances),
            (gates,),
        )
        for i, d in enumerate(distances):
            part[d] = outs[2 * i : 2 * i + 2]

    def gated(half_of, came):
        outs = sum_call(
            gates, [
                ((way * last % ep_size, ep_size), half_of[way], came[way], apart[way * last])
                for way in (1, -1)
            ],
        )
        return dict(zip((1, -1), outs))

    def add(*xs):
        return sum(x.astype(jnp.float32) for x in xs).astype(jnp.bfloat16)

    far, near = {1: 0, -1: 1}, {1: 1, -1: 0}
    moving = {way: part[reach][far[way]] for way in (1, -1)}
    late = gated(near, {1: [], -1: []})
    for d in range(last, 0, -1):
        if d < last:
            late = {way: add(late[way], part[way * d][near[way]]) for way in (1, -1)}
        compute([1 - d, d - 1] if d > 1 else [0], *moving.values())
        moving = {way: go(x, way) for way, x in moving.items()}
        late = {way: go(x, way) for way, x in late.items()}
        moving = {way: after(x, part[1 - d][0]) for way, x in moving.items()}
        if d == last:
            moving = gated(far, {way: [x] for way, x in moving.items()})
        else:
            moving = {way: add(x, part[way * d][far[way]]) for way, x in moving.items()}
    moving = {way: go(x, way) for way, x in moving.items()}
    return jnp.concatenate(
        [add(part[0][0], moving[1], late[-1]), add(part[0][1], moving[-1], late[1])]
    )


def solution(mesh):
    placed = (
        P(("grp", "ep", "dp"), None),
        P(("grp", "ep", "dp"), None),
        P(("grp", "ep", "dp"), None),
        P(("grp", "ep", "dp"), None, None),
        P(("grp", "ep", "dp"), None, None),
        P(),
        P(),
    )

    def body(tokens, expert_ids, *rest):
        devices = lax.axis_size("ep") * lax.axis_size("dp")
        gathered = devices <= 2 * expert_ids.shape[1] and 7 * devices <= LANES
        return (gathered_body if gathered else routed_body)(tokens, expert_ids, *rest)

    return jax.shard_map(
        body, mesh=mesh, in_specs=placed, out_specs=P(("grp", "ep", "dp"), None), check_vma=False
    )
```
